1024 devices in a mesh: fsdp: 128 (over y_hi, z, core), replica: 8 (over y_lo, x).
Axes of the slice: x: 4, y: 4 (y_hi: 2, y_lo: 2; y = y_hi * 2 + y_lo), z: 32, core: 2. Of those that a mesh axis runs over, the one named last changes fastest.
Arguments:
- tokens: bfloat16 [8, 16384, 4096], P('replica', 'fsdp'), may hold values from -18 to 18
- norm_gain: bfloat16 [8, 4096], P('replica'), may hold values from 0.5 to 1.5
- weight: bfloat16 [8, 4096, 512], P('replica', 'fsdp'), may hold values from -1 to 1
- cotangent: bfloat16 [8, 16384, 512], P('replica', 'fsdp'), may hold values from -8 to 8
- global_params: float32 [16, 1048576], P(None, 'fsdp'), may hold values from -6 to 6
- local_params: float32 [8, 16, 1048576], P('replica', None, 'fsdp'), may hold values from -6 to 6
- momentum: float32 [16, 1048576], P(None, 'fsdp'), may hold values from -6 to 6
- fragment: int32 [1], replicated, may hold values from 0 to 15
Outputs:
- projected: bfloat16 [8, 16384, 512], P('replica', 'fsdp')
- token_grad: bfloat16 [8, 16384, 4096], P('replica', 'fsdp')
- global_next: float32 [1048576], P('fsdp')
- momentum_next: float32 [1048576], P('fsdp')
The draws below stay inside these ranges and needn't reach their ends.
All inputs are finite; a program needn't handle non-finite values.
Results may differ from the reference program's by a relative error of at most 0.0049.
Values may be sent and summed in bfloat16 or wider, within the bound.
No kernel may reach another device: no remote copies, remote signals or barrier semaphores. Data moves between devices by JAX's collectives and lax.ppermute only.
A program may use at most 32 MiB of HBM per device.

```python
import math
import jax
import jax.numpy as jnp
from jax import lax

D = 4096
KV = 512
FRAGS = 16
REPLICAS = 8
TOKENS = 16384
FRAG_ELEMS = 1048576


def token_field(key):
    token_key = jax.random.fold_in(key, 101)
    shape = (REPLICAS, TOKENS, D)
    return jnp.clip(jax.random.normal(token_key, shape, jnp.float32), -6.0, 6.0)


def weight_field(key):
    weight_key = jax.random.fold_in(key, 103)
    values = jnp.clip(jax.random.normal(weight_key, (REPLICAS, D, KV), jnp.float32), -4.0, 4.0)
    return values * (1.0 / math.sqrt(D))


def draw_tokens(key, part):
    return token_field(key).astype(jnp.bfloat16)


def draw_weight(key, part):
    return weight_field(key).astype(jnp.bfloat16)


def draw_cotangent(key, part):
    inputs = token_field(key)
    matrices = weight_field(key)

    def one_replica(pair):
        rows, matrix = pair
        row_scale = lax.rsqrt(jnp.mean(rows * rows, axis=1, keepdims=True) + 1e-05)
        return jnp.dot(rows * row_scale, matrix, precision=lax.Precision.HIGHEST)
    aligned = lax.map(one_replica, (inputs, matrices))
    noise_key = jax.random.fold_in(key, 104)
    shape = (REPLICAS, TOKENS, KV)
    noise = jnp.clip(jax.random.normal(noise_key, shape, jnp.float32), -6.0, 6.0)
    return jnp.clip(aligned + noise, -8.0, 8.0).astype(jnp.bfloat16)


def shard_levels(rng, extent, cuts, least, largest):
    factor_of, own = 1.0, jax.random.fold_in(rng, 6)
    for axis_at, shards_of in cuts:
        heights = jnp.exp(jax.random.uniform(jax.random.fold_in(own, axis_at), (shards_of,), jnp.float32, least / len(cuts), largest / len(cuts)))
        factor_of = factor_of * jnp.repeat(heights, extent[axis_at] // shards_of).reshape([-1 if axis == axis_at else 1 for axis in range(len(extent))])
    return factor_of


def normal_values(key, dims, deviation, limit, shards=(), dtype=jnp.bfloat16):
    result = jax.random.normal(key, dims, jnp.float32) * deviation
    if len(shards) > 0:
        result = shard_levels(key, dims, shards, -0.22, 0.18) * result
    return jnp.clip(result, min=-limit, max=limit).astype(dtype)


def setup_inputs(seed: int = 0) -> dict:
    arg_keys = jax.random.split(jax.random.key(seed), 9)
    return {
        "tokens": draw_tokens(jax.random.fold_in(arg_keys[8], 71), 0),
        "norm_gain": jnp.clip(1.0 + 0.1 * jax.random.normal(arg_keys[1], (REPLICAS, D), jnp.float32), 0.5, 1.5).astype(jnp.bfloat16),
        "weight": draw_weight(jax.random.fold_in(arg_keys[8], 71), 0),
        "cotangent": draw_cotangent(jax.random.fold_in(arg_keys[8], 71), 0),
        "global_params": normal_values(arg_keys[4], (FRAGS, FRAG_ELEMS), 1.0, 6.0, ((1, 128),), jnp.float32),
        "local_params": normal_values(arg_keys[5], (REPLICAS, FRAGS, FRAG_ELEMS), 1.0, 6.0, ((0, 8), (2, 128)), jnp.float32),
        "momentum": normal_values(arg_keys[6], (FRAGS, FRAG_ELEMS), 1.0, 6.0, ((1, 128),), jnp.float32),
        "fragment": jax.random.randint(arg_keys[7], (1,), 0, FRAGS).astype(jnp.int32),
    }


epsilon = 1e-05
outer_momentum = 0.9
outer_rate = 0.7

def project_layer(inputs):
    row_block, norm_row, weight_block, upstream = inputs
    floated = row_block.astype(jnp.float32)
    inv_rms = lax.rsqrt(lax.optimization_barrier(jnp.mean(floated * floated, axis=1, keepdims=True)) + epsilon)
    unit_rows = floated * inv_rms
    gain_row = norm_row.astype(jnp.float32)
    normed = (unit_rows * gain_row).astype(jnp.bfloat16)
    projected = jnp.dot(normed, weight_block, preferred_element_type=jnp.float32).astype(jnp.bfloat16)
    grad_normed = jnp.dot(upstream, weight_block.T, preferred_element_type=jnp.float32)
    gained = grad_normed * gain_row
    inner_mean = lax.optimization_barrier(jnp.mean(gained * unit_rows, axis=1, keepdims=True))
    token_grad = (inv_rms * (gained - unit_rows * inner_mean)).astype(jnp.bfloat16)
    return (projected, token_grad)

def reference(tokens, norm_gain, weight, cotangent, global_params, local_params, momentum, fragment):
    projected, token_grad = lax.map(project_layer, (tokens, norm_gain, weight, cotangent))
    chosen = fragment[0].astype(jnp.int32)
    global_row = lax.dynamic_index_in_dim(global_params, chosen, 0, keepdims=False)
    moment_row = lax.dynamic_index_in_dim(momentum, chosen, 0, keepdims=False)
    local_rows = lax.dynamic_index_in_dim(local_params, chosen, 1, keepdims=False)
    pseudo = lax.optimization_barrier(jnp.sum(global_row[None, :] - local_rows, axis=0)) / REPLICAS
    momentum_next = outer_momentum * moment_row + pseudo
    global_next = global_row - outer_rate * (pseudo + outer_momentum * momentum_next)
    return (projected, token_grad, global_next, momentum_next)
```

```python
import functools

import jax
import jax.numpy as jnp
from jax import lax
from jax.experimental import pallas as pl
from jax.experimental.pallas import tpu as pltpu
from jax.sharding import PartitionSpec as P

epsilon = 1e-05
outer_momentum = 0.9
outer_rate = 0.7

Y, Z, C = 2, 32, 2
HOPS = (16, 8, 4, 2, 1)


def at(y, z, c):
    return (y * Z + z % Z) * C + c


def pairs(step):
    return [
        (at(y, z, c), at(*step(y, z, c)))
        for y in range(Y)
        for z in range(Z)
        for c in range(C)
    ]


def along_z(array, hop):
    return lax.ppermute(array, "fsdp", pairs(lambda y, z, c: (y, z + (hop if c == 0 else -hop), c)))


def across_y(array):
    return lax.ppermute(array, "fsdp", pairs(lambda y, z, c: (1 - y, z, c)))


def across_core(array):
    return lax.ppermute(array, "fsdp", pairs(lambda y, z, c: (y, z, 1 - c)))


def offset(slot, hops):
    return sum(hop for bit, hop in enumerate(hops) if slot >> bit & 1)


def layer_kernel(rows, layout, *refs):
    pieces = refs[: len(layout)]
    tokens, inv, gain, upstream, projected, token_grad, full, sem = refs[len(layout) :]
    place = lax.axis_index("fsdp")
    core = lax.rem(place, C)
    chip = lax.div(place, C)
    z, y = lax.rem(chip, Z), lax.div(chip, Z)
    for piece, (other_y, other_core, offsets) in zip(pieces, layout):
        owner_y = 1 - y if other_y else y
        owner_core = 1 - core if other_core else core
        sign = 2 * owner_core - 1
        for slot, moved in enumerate(offsets):
            owner_z = lax.rem(z + sign * moved + Z, Z)
            start = ((owner_y * Z + owner_z) * C + owner_core) * rows
            pltpu.make_async_copy(
                piece.at[pl.ds(slot * rows, rows)],
                full.at[pl.ds(pl.multiple_of(start, rows), rows)],
                sem,
            ).start()
    pltpu.make_async_copy(full, full, sem).wait()
    features = full.shape[0]
    chunk = 512
    total = jnp.zeros(projected.shape, jnp.float32)
    for first in range(0, features, chunk):
        cols = slice(first, first + chunk)
        unit = tokens[:, cols].astype(jnp.float32) * inv[...]
        normed = (unit * gain[:, cols].astype(jnp.float32)).astype(jnp.bfloat16)
        total += jnp.dot(normed, full[cols, :], preferred_element_type=jnp.float32)
    projected[...] = total.astype(jnp.bfloat16)
    above = upstream[...]
    inner = jnp.sum(above.astype(jnp.float32) * total, axis=1, keepdims=True) / features
    for first in range(0, features, chunk):
        cols = slice(first, first + chunk)
        grad = lax.dot_general(
            above, full[cols, :], (((1,), (1,)), ((), ())), preferred_element_type=jnp.float32
        )
        unit = tokens[:, cols].astype(jnp.float32) * inv[...]
        gained = grad * gain[:, cols].astype(jnp.float32)
        token_grad[:, cols] = (inv[...] * (gained - unit * inner)).astype(jnp.bfloat16)


def shards(tokens, norm_gain, weight, cotangent, global_params, local_params, momentum, fragment):
    chosen = fragment[0]
    global_row = lax.dynamic_index_in_dim(global_params, chosen, 0, keepdims=False)
    moment_row = lax.dynamic_index_in_dim(momentum, chosen, 0, keepdims=False)
    local_row = lax.dynamic_index_in_dim(local_params[0], chosen, 0, keepdims=False)
    difference = global_row - local_row
    replica_count = lax.axis_size("replica")
    spread = jnp.broadcast_to(difference.reshape(1, -1, 128), (replica_count, difference.size // 128, 128))
    everyone = lax.all_to_all(spread, "replica", 0, 0)
    pseudo = jnp.sum(everyone, axis=0).reshape(-1) / replica_count
    momentum_next = outer_momentum * moment_row + pseudo
    global_next = global_row - outer_rate * (pseudo + outer_momentum * momentum_next)

    own = weight[0]
    rows = own.shape[0]
    held = own
    for hop in HOPS[:-1]:
        held = jnp.concatenate([held, along_z(held, hop)], axis=0)
    last = along_z(held, HOPS[-1])
    held_y = across_y(held)
    last_y = across_y(last)
    mine = [held, held_y, last, last_y]
    other = [across_core(piece) for piece in mine]
    early = [offset(slot, HOPS[:-1]) for slot in range(2 ** (len(HOPS) - 1))]
    late = [moved + HOPS[-1] for moved in early]
    layout = [
        (other_y, other_core, offsets)
        for other_core in (False, True)
        for offsets in (early, late)
        for other_y in (False, True)
    ]
    block = tokens[0]
    floated = block.astype(jnp.float32)
    inv = lax.rsqrt(jnp.mean(floated * floated, axis=1, keepdims=True) + epsilon)
    count, features = block.shape
    width = own.shape[1]
    vmem = pl.BlockSpec(memory_space=pltpu.VMEM)
    projected, token_grad = pl.pallas_call(
        functools.partial(layer_kernel, rows, layout),
        out_shape=(
            jax.ShapeDtypeStruct((count, width), jnp.bfloat16),
            jax.ShapeDtypeStruct((count, features), jnp.bfloat16),
        ),
        in_specs=[pl.BlockSpec(memory_space=pl.ANY)] * len(layout) + [vmem] * 4,
        out_specs=(vmem, vmem),
        scratch_shapes=[pltpu.VMEM((features, width), jnp.bfloat16), pltpu.SemaphoreType.DMA],
        compiler_params=pltpu.CompilerParams(vmem_limit_bytes=24 * 2**20),
        cost_estimate=pl.CostEstimate(flops=4 * count * features * width, bytes_accessed=8 * 2**20, transcendentals=0),
    )(*mine, *other, block, inv, norm_gain, cotangent[0])
    return (projected[None], token_grad[None], global_next, momentum_next)


def solution(mesh):
    placed = (
        P("replica", "fsdp", None),
        P("replica", None),
        P("replica", "fsdp", None),
        P("replica", "fsdp", None),
        P(None, "fsdp"),
        P("replica", None, "fsdp"),
        P(None, "fsdp"),
        P(),
    )
    return jax.shard_map(
        shards,
        mesh=mesh,
        in_specs=placed,
        out_specs=(P("replica", "fsdp", None), P("replica", "fsdp", None), P("fsdp"), P("fsdp")),
        check_vma=False,
    )
```

```python
import functools

import jax
import jax.numpy as jnp
from jax import lax
from jax.experimental import pallas as pl
from jax.experimental.pallas import tpu as pltpu
from jax.sharding import PartitionSpec as P

epsilon = 1e-05
outer_momentum = 0.9
outer_rate = 0.7

Y, Z, C = 2, 32, 2
VMEM = pl.BlockSpec(memory_space=pltpu.VMEM)
SMEM = pl.BlockSpec(memory_space=pltpu.SMEM)
ANY = pl.BlockSpec(memory_space=pl.ANY)


def at(y, z, c):
    return (y * Z + z % Z) * C + c


def sources():
    return [(y, z, c) for y in range(Y) for z in range(Z) for c in range(C)]


def send(array, step):
    return lax.ppermute(array, "fsdp", [(at(*here), at(*step(*here))) for here in sources()])


def along_z(array, hop):
    return send(array, lambda y, z, c: (y, z + (hop if c == 0 else -hop), c))


def across_y(array):
    return send(array, lambda y, z, c: (1 - y, z, c))


def across_core(array):
    return send(array, lambda y, z, c: (y, z, 1 - c))


def chip_kernel(own, first, second, out):
    rows = own.shape[0]
    core = lax.rem(lax.axis_index("fsdp"), C)

    @pl.when(core == 0)
    def _():
        out[:rows, :] = own[...]
        out[rows:, :] = first[...]

    @pl.when(core != 0)
    def _():
        out[:rows, :] = first[...]
        out[rows:, :] = second[...]


def chip_rows(own):
    first = send(own, lambda y, z, c: (y, z - 1, 1) if c == 0 else (y, z, 0))
    down = [(at(y, z, c), at(y, z - 1, c)) for y, z, c in sources() if c == 1]
    second = lax.ppermute(own, "fsdp", down)
    rows, width = own.shape
    return pl.pallas_call(
        chip_kernel,
        out_shape=jax.ShapeDtypeStruct((C * rows, width), own.dtype),
        in_specs=[VMEM] * 3,
        out_specs=VMEM,
        compiler_params=pltpu.CompilerParams(vmem_limit_bytes=2**20),
    )(own, first, second)


def join_kernel(first, second, *refs):
    out, rows = refs[-1], first.shape[0]
    out[:rows, :] = first[...]
    out[rows:, :] = second[...]


def join(first, second, *ahead, flops=0):
    rows, width = first.shape
    return pl.pallas_call(
        join_kernel,
        out_shape=jax.ShapeDtypeStruct((2 * rows, width), first.dtype),
        in_specs=[VMEM] * 2 + [ANY] * len(ahead),
        out_specs=VMEM,
        compiler_params=pltpu.CompilerParams(vmem_limit_bytes=4 * 2**20),
        cost_estimate=pl.CostEstimate(flops=flops, bytes_accessed=4 * rows * width, transcendentals=0),
    )(first, second, *ahead)


def pick_kernel(chosen, params, local, momentum, ahead, spread, params_row, moment_row, held, sems):
    index = chosen[0]
    group = pl.multiple_of(lax.div(index, 8) * 8, 8)
    row = lax.rem(index, 8)
    copies = [
        pltpu.make_async_copy(source.at[pl.ds(group, 8)], held.at[slot], sems.at[slot])
        for slot, source in enumerate((params, local, momentum))
    ]
    for copy in copies:
        copy.start()
    for copy in copies:
        copy.wait()
    wanted = lax.broadcasted_iota(jnp.int32, (8, 128), 0) == row

    def taken(slot, lanes):
        return jnp.sum(jnp.where(wanted, held[slot, :, lanes], 0.0), axis=0, keepdims=True)

    for line in range(params_row.shape[0]):
        lanes = slice(128 * line, 128 * line + 128)
        mine = taken(0, lanes)
        spread[:, line, :] = jnp.broadcast_to(mine - taken(1, lanes), (spread.shape[0], 128))
        params_row[line : line + 1, :] = mine
        moment_row[line : line + 1, :] = taken(2, lanes)


def pick(fragment, params, local, momentum, replicas, ahead):
    length = params.shape[1]
    lines = length // 128
    row = jax.ShapeDtypeStruct((lines, 128), jnp.float32)
    return pl.pallas_call(
        pick_kernel,
        out_shape=(jax.ShapeDtypeStruct((replicas, lines, 128), jnp.float32), row, row),
        in_specs=[SMEM] + [ANY] * 4,
        out_specs=(VMEM,) * 3,
        scratch_shapes=[pltpu.VMEM((3, 8, length), jnp.float32), pltpu.SemaphoreType.DMA((3,))],
        compiler_params=pltpu.CompilerParams(vmem_limit_bytes=4 * 2**20),
    )(fragment, params, local, momentum, ahead)


def side_kernel(everyone, params_row, moment_row, tokens, params_next, moment_next, inv):
    count = everyone.shape[0]
    total = everyone[0]
    for replica in range(1, count):
        total = total + everyone[replica]
    pseudo = total / count
    moment = outer_momentum * moment_row[...] + pseudo
    moment_next[...] = moment
    params_next[...] = params_row[...] - outer_rate * (pseudo + outer_momentum * moment)
    features = tokens.shape[1]
    squares = jnp.zeros(inv.shape, jnp.float32)
    for first in range(0, features, 512):
        floated = tokens[:, first : first + 512].astype(jnp.float32)
        squares = squares + jnp.sum(floated * floated, axis=1, keepdims=True)
    inv[...] = lax.rsqrt(squares / features + epsilon)


def side(everyone, params_row, moment_row, tokens):
    row = jax.ShapeDtypeStruct(params_row.shape, jnp.float32)
    return pl.pallas_call(
        side_kernel,
        out_shape=(row, row, jax.ShapeDtypeStruct((tokens.shape[0], 1), jnp.float32)),
        in_specs=[VMEM] * 4,
        out_specs=(VMEM,) * 3,
        compiler_params=pltpu.CompilerParams(vmem_limit_bytes=4 * 2**20),
    )(everyone, params_row, moment_row, tokens)


def layer_kernel(rows, layout, *refs):
    pieces = refs[: len(layout)]
    tokens, inv, gain, cotangent, projected, token_grad, full, staged, upstream, sems = refs[len(layout) :]
    fetch = pltpu.make_async_copy(cotangent, upstream, sems.at[len(layout)])
    fetch.start()
    loads, first = [], 0
    for number, piece in enumerate(pieces):
        target = staged.at[pl.ds(first, piece.shape[0])]
        loads.append((first, pltpu.make_async_copy(piece, target, sems.at[number])))
        loads[-1][1].start()
        first += piece.shape[0]
    place = lax.axis_index("fsdp")
    core = lax.rem(place, C)
    chip = lax.div(place, C)
    z, y = lax.rem(chip, Z), lax.div(chip, Z)
    for (first, load), (other_y, other_core, offsets) in zip(loads, layout):
        owner_y = 1 - y if other_y else y
        owner_core = 1 - core if other_core else core
        load.wait()
        for slot, moved in enumerate(offsets):
            owner_z = lax.rem(z + Z + jnp.where(owner_core == 0, -moved, moved + 1), Z)
            start = pl.multiple_of((owner_y * Z + owner_z) * rows, rows)
            full[pl.ds(start, rows), :] = staged[first + slot * rows : first + (slot + 1) * rows, :]
    features = full.shape[0]
    chunk = 512
    total = jnp.zeros(projected.shape, jnp.float32)
    for first in range(0, features, chunk):
        cols = slice(first, first + chunk)
        unit = tokens[:, cols].astype(jnp.float32) * inv[...]
        normed = (unit * gain[:, cols].astype(jnp.float32)).astype(jnp.bfloat16)
        total += jnp.dot(normed, full[cols, :], preferred_element_type=jnp.float32)
    projected[...] = total.astype(jnp.bfloat16)
    fetch.wait()
    above = upstream[...]
    inner = jnp.sum(above.astype(jnp.float32) * total, axis=1, keepdims=True) / features
    for first in range(0, features, chunk):
        cols = slice(first, first + chunk)
        grad = lax.dot_general(
            above, full[cols, :], (((1,), (1,)), ((), ())), preferred_element_type=jnp.float32
        )
        unit = tokens[:, cols].astype(jnp.float32) * inv[...]
        gained = grad * gain[:, cols].astype(jnp.float32)
        token_grad[:, cols] = (inv[...] * (gained - unit * inner)).astype(jnp.bfloat16)


def shards(tokens, norm_gain, weight, cotangent, global_params, local_params, momentum, fragment):
    own = weight[0]
    rows = C * own.shape[0]
    block = tokens[0]
    one = chip_rows(own)
    spread, params_row, moment_row = pick(
        fragment, global_params, local_params[0], momentum, lax.axis_size("replica"), one
    )
    next_one = along_z(one, 8)
    everyone = lax.all_to_all(spread, "replica", 0, 0)
    two = join(one, next_one, flops=10**10)
    next_two = along_z(two, 4)
    global_next, momentum_next, inv = side(everyone, params_row, moment_row, block)
    four = join(two, next_two, inv)
    next_four = along_z(four, 2)
    four_y = across_y(four)
    eight = join(four, next_four, flops=10**10)
    next_four_y = across_y(next_four)
    last = along_z(eight, 1)
    eight_c = across_core(eight)
    eight_y = join(four_y, next_four_y)
    last_y = along_z(eight_y, 1)
    before = (0, 8, 4, 12, 2, 10, 6, 14)
    after = tuple(moved + 1 for moved in before)
    gathered = [
        (eight, False, False, before),
        (eight_c, False, True, before),
        (eight_y, True, False, before),
        (last, False, False, after),
        (across_core(eight_y), True, True, before),
        (across_core(last), False, True, after),
        (last_y, True, False, after),
        (across_core(last_y), True, True, after),
    ]
    layout = [entry[1:] for entry in gathered]
    count, features = block.shape
    width = own.shape[1]
    projected, token_grad = pl.pallas_call(
        functools.partial(layer_kernel, rows, layout),
        out_shape=(
            jax.ShapeDtypeStruct((count, width), jnp.bfloat16),
            jax.ShapeDtypeStruct((count, features), jnp.bfloat16),
        ),
        in_specs=[ANY] * len(layout) + [VMEM] * 3 + [ANY],
        out_specs=(VMEM, VMEM),
        scratch_shapes=[
            pltpu.VMEM((features, width), jnp.bfloat16),
            pltpu.VMEM((features, width), jnp.bfloat16),
            pltpu.VMEM((count, width), jnp.bfloat16),
            pltpu.SemaphoreType.DMA((len(layout) + 1,)),
        ],
        compiler_params=pltpu.CompilerParams(vmem_limit_bytes=16 * 2**20),
        cost_estimate=pl.CostEstimate(flops=4 * count * features * width, bytes_accessed=8 * 2**20, transcendentals=0),
    )(*[entry[0] for entry in gathered], block, inv, norm_gain, cotangent[0])
    return (projected[None], token_grad[None], global_next.reshape(-1), momentum_next.reshape(-1))


def solution(mesh):
    placed = (
        P("replica", "fsdp", None),
        P("replica", None),
        P("replica", "fsdp", None),
        P("replica", "fsdp", None),
        P(None, "fsdp"),
        P("replica", None, "fsdp"),
        P(None, "fsdp"),
        P(),
    )
    return jax.shard_map(
        shards,
        mesh=mesh,
        in_specs=placed,
        out_specs=(P("replica", "fsdp", None), P("replica", "fsdp", None), P("fsdp"), P("fsdp")),
        check_vma=False,
    )
```

```python
import functools

import jax
import jax.numpy as jnp
from jax import lax
from jax.experimental import pallas as pl
from jax.experimental.pallas import tpu as pltpu
from jax.sharding import PartitionSpec as P

epsilon = 1e-05
outer_momentum = 0.9
outer_rate = 0.7

Y, Z, C = 2, 32, 2
VMEM = pl.BlockSpec(memory_space=pltpu.VMEM)
SMEM = pl.BlockSpec(memory_space=pltpu.SMEM)
ANY = pl.BlockSpec(memory_space=pl.ANY)


def at(y, z, c):
    return (y * Z + z % Z) * C + c


def sources():
    return [(y, z, c) for y in range(Y) for z in range(Z) for c in range(C)]


def send(array, step):
    return lax.ppermute(array, "fsdp", [(at(*here), at(*step(*here))) for here in sources()])


def along_z(array, hop):
    return send(array, lambda y, z, c: (y, z + (hop if c == 0 else -hop), c))


def across_y(array):
    return send(array, lambda y, z, c: (1 - y, z, c))


def across_core(array):
    return send(array, lambda y, z, c: (y, z, 1 - c))


def chip_kernel(first, second, out):
    rows = first.shape[0]
    core = lax.rem(lax.axis_index("fsdp"), C)

    @pl.when(core == 0)
    def _():
        out[:rows, :] = second[...]
        out[rows:, :] = first[...]

    @pl.when(core != 0)
    def _():
        out[:rows, :] = first[...]
        out[rows:, :] = second[...]


def chip_rows(own):
    first = send(own, lambda y, z, c: (y, z - 1, 1) if c == 0 else (y, z, 0))
    second = send(own, lambda y, z, c: (y, z - c, c))
    rows, width = own.shape
    return pl.pallas_call(
        chip_kernel,
        out_shape=jax.ShapeDtypeStruct((C * rows, width), own.dtype),
        in_specs=[VMEM] * 2,
        out_specs=VMEM,
        compiler_params=pltpu.CompilerParams(vmem_limit_bytes=2**20),
    )(first, second)


def join_kernel(first, second, *refs):
    out, rows = refs[-1], first.shape[0]
    out[:rows, :] = first[...]
    out[rows:, :] = second[...]


def join(first, second, *ahead, flops=0):
    rows, width = first.shape
    return pl.pallas_call(
        join_kernel,
        out_shape=jax.ShapeDtypeStruct((2 * rows, width), first.dtype),
        in_specs=[VMEM] * 2 + [ANY] * len(ahead),
        out_specs=VMEM,
        compiler_params=pltpu.CompilerParams(vmem_limit_bytes=4 * 2**20),
        cost_estimate=pl.CostEstimate(flops=flops, bytes_accessed=4 * rows * width, transcendentals=0),
    )(first, second, *ahead)


def pick_kernel(chosen, params, local, momentum, ahead, spread, params_row, moment_row, held, sems):
    index = chosen[0]
    group = pl.multiple_of(lax.div(index, 8) * 8, 8)
    row = lax.rem(index, 8)
    copies = [
        pltpu.make_async_copy(source.at[pl.ds(group, 8)], held.at[slot], sems.at[slot])
        for slot, source in enumerate((params, local, momentum))
    ]
    for copy in copies:
        copy.start()
    for copy in copies:
        copy.wait()
    wanted = lax.broadcasted_iota(jnp.int32, (8, 128), 0) == row

    def taken(slot, lanes):
        return jnp.sum(jnp.where(wanted, held[slot, :, lanes], 0.0), axis=0, keepdims=True)

    for line in range(params_row.shape[0]):
        lanes = slice(128 * line, 128 * line + 128)
        mine = taken(0, lanes)
        spread[:, line, :] = jnp.broadcast_to(mine - taken(1, lanes), (spread.shape[0], 128))
        params_row[line : line + 1, :] = mine
        moment_row[line : line + 1, :] = taken(2, lanes)


def pick(fragment, params, local, momentum, replicas, ahead):
    length = params.shape[1]
    lines = length // 128
    row = jax.ShapeDtypeStruct((lines, 128), jnp.float32)
    return pl.pallas_call(
        pick_kernel,
        out_shape=(jax.ShapeDtypeStruct((replicas, lines, 128), jnp.float32), row, row),
        in_specs=[SMEM] + [ANY] * 4,
        out_specs=(VMEM,) * 3,
        scratch_shapes=[pltpu.VMEM((3, 8, length), jnp.float32), pltpu.SemaphoreType.DMA((3,))],
        compiler_params=pltpu.CompilerParams(vmem_limit_bytes=60 * 2**20),
    )(fragment, params, local, momentum, ahead)


def side_kernel(everyone, params_row, moment_row, tokens, params_next, moment_next, inv):
    count = everyone.shape[0]
    total = everyone[0]
    for replica in range(1, count):
        total = total + everyone[replica]
    pseudo = total / count
    moment = outer_momentum * moment_row[...] + pseudo
    moment_next[...] = moment
    params_next[...] = params_row[...] - outer_rate * (pseudo + outer_momentum * moment)
    features = tokens.shape[1]
    squares = jnp.zeros(inv.shape, jnp.float32)
    for first in range(0, features, 512):
        floated = tokens[:, first : first + 512].astype(jnp.float32)
        squares = squares + jnp.sum(floated * floated, axis=1, keepdims=True)
    inv[...] = lax.rsqrt(squares / features + epsilon)


def side(everyone, params_row, moment_row, tokens):
    row = jax.ShapeDtypeStruct(params_row.shape, jnp.float32)
    return pl.pallas_call(
        side_kernel,
        out_shape=(row, row, jax.ShapeDtypeStruct((tokens.shape[0], 1), jnp.float32)),
        in_specs=[VMEM] * 4,
        out_specs=(VMEM,) * 3,
        compiler_params=pltpu.CompilerParams(vmem_limit_bytes=4 * 2**20),
    )(everyone, params_row, moment_row, tokens)


def position():
    place = lax.axis_index("fsdp")
    chip = lax.div(place, C)
    return lax.div(chip, Z), lax.rem(chip, Z), lax.rem(place, C)


def put(piece, full, rows, other_core, offsets):
    _, z, core = position()
    owner_core = 1 - core if other_core else core
    for slot, moved in enumerate(offsets):
        owner_z = lax.rem(z + Z + jnp.where(owner_core == 0, -moved, moved + 1), Z)
        start = pl.multiple_of(owner_z * rows, rows)
        full[pl.ds(start, rows), :] = piece[slot * rows : (slot + 1) * rows, :]


def lanes_of(column, half, first, chunk):
    return pl.ds(pl.multiple_of(column * half + first, 128), chunk)


CHUNK = 512


def forward(tokens, inv, gain, full, column, total):
    for first in range(0, full.shape[0], CHUNK):
        lanes = lanes_of(column, full.shape[0], first, CHUNK)
        unit = tokens[:, lanes].astype(jnp.float32) * inv[...]
        normed = (unit * gain[:, lanes].astype(jnp.float32)).astype(jnp.bfloat16)
        total += jnp.dot(normed, full[first : first + CHUNK, :], preferred_element_type=jnp.float32)
    return total


def gained_of(upstream, gain, full, column, first):
    grad = lax.dot_general(
        upstream, full[first : first + CHUNK, :], (((1,), (1,)), ((), ())), preferred_element_type=jnp.float32
    )
    return grad * gain[:, lanes_of(column, full.shape[0], first, CHUNK)].astype(jnp.float32)


def own_kernel(rows, layout, *refs):
    pieces = refs[: len(layout)]
    tokens, inv, gain, upstream, partial, gained, full = refs[len(layout) :]
    for piece, (other_core, offsets) in zip(pieces, layout):
        put(piece, full, rows, other_core, offsets)
    y, _, _ = position()
    partial[...] = forward(tokens, inv, gain, full, y, jnp.zeros(partial.shape, jnp.float32))
    for first in range(0, full.shape[0], CHUNK):
        gained[:, first : first + CHUNK] = gained_of(upstream[...], gain, full, y, first)


def other_kernel(rows, layout, *refs):
    pieces = refs[: len(layout)]
    tokens, inv, gain, upstream, partial, gained, projected, token_grad, full = refs[len(layout) :]
    for piece, (other_core, offsets) in zip(pieces, layout):
        put(piece, full, rows, other_core, offsets)
    y, _, _ = position()
    total = forward(tokens, inv, gain, full, 1 - y, partial[...])
    projected[...] = total.astype(jnp.bfloat16)
    above = upstream[...]
    inner = jnp.sum(above.astype(jnp.float32) * total, axis=1, keepdims=True) / tokens.shape[1]

    def finish(column, first, values):
        lanes = lanes_of(column, full.shape[0], first, CHUNK)
        unit = tokens[:, lanes].astype(jnp.float32) * inv[...]
        token_grad[:, lanes] = (inv[...] * (values - unit * inner)).astype(jnp.bfloat16)

    for first in range(0, full.shape[0], CHUNK):
        finish(1 - y, first, gained_of(above, gain, full, 1 - y, first))
        finish(y, first, gained[:, first : first + CHUNK])


def shards(tokens, norm_gain, weight, cotangent, global_params, local_params, momentum, fragment):
    own = weight[0]
    rows = C * own.shape[0]
    block = tokens[0]
    one = chip_rows(own)
    spread, params_row, moment_row = pick(
        fragment, global_params, local_params[0], momentum, lax.axis_size("replica"), one
    )
    next_one = along_z(one, 8)
    everyone = lax.all_to_all(spread, "replica", 0, 0)
    two = join(one, next_one, flops=10**10)
    next_two = along_z(two, 4)
    global_next, momentum_next, inv = side(everyone, params_row, moment_row, block)
    four = join(two, next_two, inv)
    next_four = along_z(four, 2)
    four_y = across_y(four)
    eight = join(four, next_four, flops=10**10)
    next_four_y = across_y(next_four)
    last = along_z(eight, 1)
    eight_c = across_core(eight)
    eight_y = join(four_y, next_four_y)
    last_y = along_z(eight_y, 1)
    before = (0, 8, 4, 12, 2, 10, 6, 14)
    after = tuple(moved + 1 for moved in before)
    count, features = block.shape
    width = own.shape[1]
    half = features // Y
    layout = [(False, before), (True, before), (False, after), (True, after)]
    scratch = [pltpu.VMEM((half, width), jnp.bfloat16)]
    params = pltpu.CompilerParams(vmem_limit_bytes=8 * 2**20)
    flops = 2 * count * features * width
    cost = pl.CostEstimate(flops=flops, bytes_accessed=4 * 2**20, transcendentals=0)
    partial, gained = pl.pallas_call(
        functools.partial(own_kernel, rows, layout),
        out_shape=(
            jax.ShapeDtypeStruct((count, width), jnp.float32),
            jax.ShapeDtypeStruct((count, half), jnp.float32),
        ),
        in_specs=[VMEM] * (len(layout) + 4),
        out_specs=(VMEM, VMEM),
        scratch_shapes=scratch,
        compiler_params=params,
        cost_estimate=cost,
    )(eight, eight_c, last, across_core(last), block, inv, norm_gain, cotangent[0])
    projected, token_grad = pl.pallas_call(
        functools.partial(other_kernel, rows, layout),
        out_shape=(
            jax.ShapeDtypeStruct((count, width), jnp.bfloat16),
            jax.ShapeDtypeStruct((count, features), jnp.bfloat16),
        ),
        in_specs=[VMEM] * (len(layout) + 6),
        out_specs=(VMEM, VMEM),
        scratch_shapes=scratch,
        compiler_params=params,
        cost_estimate=cost,
    )(
        *(eight_y, across_core(eight_y), last_y, across_core(last_y)),
        *(block, inv, norm_gain, cotangent[0], partial, gained),
    )
    return (projected[None], token_grad[None], global_next.reshape(-1), momentum_next.reshape(-1))


def solution(mesh):
    placed = (
        P("replica", "fsdp", None),
        P("replica", None),
        P("replica", "fsdp", None),
        P("replica", "fsdp", None),
        P(None, "fsdp"),
        P("replica", None, "fsdp"),
        P(None, "fsdp"),
        P(),
    )
    return jax.shard_map(
        shards,
        mesh=mesh,
        in_specs=placed,
        out_specs=(P("replica", "fsdp", None), P("replica", "fsdp", None), P("fsdp"), P("fsdp")),
        check_vma=False,
    )
```

```python
import functools

import jax
import jax.numpy as jnp
from jax import lax
from jax.experimental import pallas as pl
from jax.experimental.pallas import tpu as pltpu
from jax.sharding import PartitionSpec as P

epsilon = 1e-05
outer_momentum = 0.9
outer_rate = 0.7

Y, Z, C = 2, 32, 2
VMEM = pl.BlockSpec(memory_space=pltpu.VMEM)
SMEM = pl.BlockSpec(memory_space=pltpu.SMEM)
ANY = pl.BlockSpec(memory_space=pl.ANY)


def at(y, z, c):
    return (y * Z + z % Z) * C + c


def sources():
    return [(y, z, c) for y in range(Y) for z in range(Z) for c in range(C)]


def send(array, step):
    return lax.ppermute(array, "fsdp", [(at(*here), at(*step(*here))) for here in sources()])


def along_z(array, hop):
    return send(array, lambda y, z, c: (y, z + (hop if c == 0 else -hop), c))


def across_y(array):
    return send(array, lambda y, z, c: (1 - y, z, c))


def across_core(array):
    return send(array, lambda y, z, c: (y, z, 1 - c))


def chip_kernel(first, second, out):
    rows = first.shape[0]
    core = lax.rem(lax.axis_index("fsdp"), C)

    @pl.when(core == 0)
    def _():
        out[:rows, :] = second[...]
        out[rows:, :] = first[...]

    @pl.when(core != 0)
    def _():
        out[:rows, :] = first[...]
        out[rows:, :] = second[...]


def chip_rows(own):
    first = send(own, lambda y, z, c: (y, z - 1, 1) if c == 0 else (y, z, 0))
    second = send(own, lambda y, z, c: (y, z - c, c))
    rows, width = own.shape
    return pl.pallas_call(
        chip_kernel,
        out_shape=jax.ShapeDtypeStruct((C * rows, width), own.dtype),
        in_specs=[VMEM] * 2,
        out_specs=VMEM,
        compiler_params=pltpu.CompilerParams(vmem_limit_bytes=2**20),
    )(first, second)


def join_kernel(parts, *refs):
    out, first = refs[-1], 0
    for part in refs[:parts]:
        out[first : first + part.shape[0], :] = part[...]
        first += part.shape[0]


def join(parts, *ahead, flops=0):
    rows = sum(part.shape[0] for part in parts)
    width = parts[0].shape[1]
    return pl.pallas_call(
        functools.partial(join_kernel, len(parts)),
        out_shape=jax.ShapeDtypeStruct((rows, width), parts[0].dtype),
        in_specs=[VMEM] * len(parts) + [ANY] * len(ahead),
        out_specs=VMEM,
        compiler_params=pltpu.CompilerParams(vmem_limit_bytes=4 * 2**20),
        cost_estimate=pl.CostEstimate(flops=flops, bytes_accessed=4 * rows * width, transcendentals=0),
    )(*parts, *ahead)


def pick_kernel(chosen, params, local, momentum, ahead, spread, params_row, moment_row, held, sems):
    index = chosen[0]
    group = pl.multiple_of(lax.div(index, 8) * 8, 8)
    row = lax.rem(index, 8)
    copies = [
        pltpu.make_async_copy(source.at[pl.ds(group, 8)], held.at[slot], sems.at[slot])
        for slot, source in enumerate((params, local, momentum))
    ]
    for copy in copies:
        copy.start()
    for copy in copies:
        copy.wait()
    wanted = lax.broadcasted_iota(jnp.int32, (8, 128), 0) == row

    def taken(slot, lanes):
        return jnp.sum(jnp.where(wanted, held[slot, :, lanes], 0.0), axis=0, keepdims=True)

    for line in range(params_row.shape[0]):
        lanes = slice(128 * line, 128 * line + 128)
        mine = taken(0, lanes)
        spread[:, line, :] = jnp.broadcast_to(mine - taken(1, lanes), (spread.shape[0], 128))
        params_row[line : line + 1, :] = mine
        moment_row[line : line + 1, :] = taken(2, lanes)


def pick(fragment, params, local, momentum, replicas, ahead):
    length = params.shape[1]
    lines = length // 128
    row = jax.ShapeDtypeStruct((lines, 128), jnp.float32)
    return pl.pallas_call(
        pick_kernel,
        out_shape=(jax.ShapeDtypeStruct((replicas, lines, 128), jnp.float32), row, row),
        in_specs=[SMEM] + [ANY] * 4,
        out_specs=(VMEM,) * 3,
        scratch_shapes=[pltpu.VMEM((3, 8, length), jnp.float32), pltpu.SemaphoreType.DMA((3,))],
        compiler_params=pltpu.CompilerParams(vmem_limit_bytes=4 * 2**20),
    )(fragment, params, local, momentum, ahead)


def side_kernel(everyone, params_row, moment_row, tokens, params_next, moment_next, inv):
    count = everyone.shape[0]
    total = everyone[0]
    for replica in range(1, count):
        total = total + everyone[replica]
    pseudo = total / count
    moment = outer_momentum * moment_row[...] + pseudo
    moment_next[...] = moment
    params_next[...] = params_row[...] - outer_rate * (pseudo + outer_momentum * moment)
    features = tokens.shape[1]
    squares = jnp.zeros(inv.shape, jnp.float32)
    for first in range(0, features, 512):
        floated = tokens[:, first : first + 512].astype(jnp.float32)
        squares = squares + jnp.sum(floated * floated, axis=1, keepdims=True)
    inv[...] = lax.rsqrt(squares / features + epsilon)


def side(everyone, params_row, moment_row, tokens):
    row = jax.ShapeDtypeStruct(params_row.shape, jnp.float32)
    return pl.pallas_call(
        side_kernel,
        out_shape=(row, row, jax.ShapeDtypeStruct((tokens.shape[0], 1), jnp.float32)),
        in_specs=[VMEM] * 4,
        out_specs=(VMEM,) * 3,
        compiler_params=pltpu.CompilerParams(vmem_limit_bytes=4 * 2**20),
    )(everyone, params_row, moment_row, tokens)


def position():
    place = lax.axis_index("fsdp")
    chip = lax.div(place, C)
    return lax.div(chip, Z), lax.rem(chip, Z), lax.rem(place, C)


def put(piece, full, rows, other_core, offsets):
    _, z, core = position()
    owner_core = 1 - core if other_core else core
    for slot, moved in enumerate(offsets):
        owner_z = lax.rem(z + Z + jnp.where(owner_core == 0, -moved, moved + 1), Z)
        start = pl.multiple_of(owner_z * rows, rows)
        full[pl.ds(start, rows), :] = piece[slot * rows : (slot + 1) * rows, :]


def lanes_of(column, half, first, chunk):
    return pl.ds(pl.multiple_of(column * half + first, 128), chunk)


CHUNK = 512


def forward(tokens, inv, gain, full, column, total):
    for first in range(0, full.shape[0], CHUNK):
        lanes = lanes_of(column, full.shape[0], first, CHUNK)
        unit = tokens[:, lanes].astype(jnp.float32) * inv[...]
        normed = (unit * gain[:, lanes].astype(jnp.float32)).astype(jnp.bfloat16)
        total += jnp.dot(normed, full[first : first + CHUNK, :], preferred_element_type=jnp.float32)
    return total


def gained_of(upstream, gain, full, column, first):
    grad = lax.dot_general(
        upstream, full[first : first + CHUNK, :], (((1,), (1,)), ((), ())), preferred_element_type=jnp.float32
    )
    return grad * gain[:, lanes_of(column, full.shape[0], first, CHUNK)].astype(jnp.float32)


def own_kernel(rows, layout, *refs):
    pieces = refs[: len(layout)]
    tokens, inv, gain, upstream, partial, gained, full = refs[len(layout) :]
    for piece, (other_core, offsets) in zip(pieces, layout):
        put(piece, full, rows, other_core, offsets)
    y, _, _ = position()
    partial[...] = forward(tokens, inv, gain, full, y, jnp.zeros(partial.shape, jnp.float32))
    for first in range(0, full.shape[0], CHUNK):
        gained[:, first : first + CHUNK] = gained_of(upstream[...], gain, full, y, first)


def other_kernel(rows, layout, *refs):
    pieces = refs[: len(layout)]
    tokens, inv, gain, upstream, partial, gained, projected, token_grad, full = refs[len(layout) :]
    for piece, (other_core, offsets) in zip(pieces, layout):
        put(piece, full, rows, other_core, offsets)
    y, _, _ = position()
    total = forward(tokens, inv, gain, full, 1 - y, partial[...])
    projected[...] = total.astype(jnp.bfloat16)
    above = upstream[...]
    inner = jnp.sum(above.astype(jnp.float32) * total, axis=1, keepdims=True) / tokens.shape[1]

    def finish(column, first, values):
        lanes = lanes_of(column, full.shape[0], first, CHUNK)
        unit = tokens[:, lanes].astype(jnp.float32) * inv[...]
        token_grad[:, lanes] = (inv[...] * (values - unit * inner)).astype(jnp.bfloat16)

    for first in range(0, full.shape[0], CHUNK):
        finish(1 - y, first, gained_of(above, gain, full, 1 - y, first))
        finish(y, first, gained[:, first : first + CHUNK])


def shards(tokens, norm_gain, weight, cotangent, global_params, local_params, momentum, fragment):
    own = weight[0]
    rows = C * own.shape[0]
    block = tokens[0]
    one = chip_rows(own)
    spread, params_row, moment_row = pick(
        fragment, global_params, local_params[0], momentum, lax.axis_size("replica"), one
    )
    everyone = lax.all_to_all(spread, "replica", 0, 0)
    next_one = along_z(one, 8)
    two = join((one, next_one), spread, flops=10**10)
    next_two = along_z(two, 4)
    early = along_z(two, 2)
    global_next, momentum_next, inv = side(everyone, params_row, moment_row, block)
    late = along_z(next_two, 2)
    four = join((two, next_two), inv)
    four_y = across_y(four)
    next_four = join((early, late), flops=10**10)
    next_four_y = across_y(next_four)
    eight = join((four, next_four))
    last = along_z(eight, 1)
    eight_c = across_core(eight)
    eight_y = join((four_y, next_four_y))
    last_y = along_z(eight_y, 1)
    before = (0, 8, 4, 12, 2, 10, 6, 14)
    behind = tuple(moved + 1 for moved in before)
    count, features = block.shape
    width = own.shape[1]
    half = features // Y
    layout = [(False, before), (True, before), (False, behind), (True, behind)]
    scratch = [pltpu.VMEM((half, width), jnp.bfloat16)]
    params = pltpu.CompilerParams(vmem_limit_bytes=8 * 2**20)
    flops = 2 * count * features * width
    cost = pl.CostEstimate(flops=flops, bytes_accessed=4 * 2**20, transcendentals=0)
    partial, gained = pl.pallas_call(
        functools.partial(own_kernel, rows, layout),
        out_shape=(
            jax.ShapeDtypeStruct((count, width), jnp.float32),
            jax.ShapeDtypeStruct((count, half), jnp.float32),
        ),
        in_specs=[VMEM] * (len(layout) + 4),
        out_specs=(VMEM, VMEM),
        scratch_shapes=scratch,
        compiler_params=params,
        cost_estimate=cost,
    )(eight, eight_c, last, across_core(last), block, inv, norm_gain, cotangent[0])
    projected, token_grad = pl.pallas_call(
        functools.partial(other_kernel, rows, layout),
        out_shape=(
            jax.ShapeDtypeStruct((count, width), jnp.bfloat16),
            jax.ShapeDtypeStruct((count, features), jnp.bfloat16),
        ),
        in_specs=[VMEM] * (len(layout) + 6),
        out_specs=(VMEM, VMEM),
        scratch_shapes=scratch,
        compiler_params=params,
        cost_estimate=cost,
    )(
        *(eight_y, across_core(eight_y), last_y, across_core(last_y)),
        *(block, inv, norm_gain, cotangent[0], partial, gained),
    )
    return (projected[None], token_grad[None], global_next.reshape(-1), momentum_next.reshape(-1))


def solution(mesh):
    placed = (
        P("replica", "fsdp", None),
        P("replica", None),
        P("replica", "fsdp", None),
        P("replica", "fsdp", None),
        P(None, "fsdp"),
        P("replica", None, "fsdp"),
        P(None, "fsdp"),
        P(),
    )
    return jax.shard_map(
        shards,
        mesh=mesh,
        in_specs=placed,
        out_specs=(P("replica", "fsdp", None), P("replica", "fsdp", None), P("fsdp"), P("fsdp")),
        check_vma=False,
    )
```

```python
import functools

import jax
import jax.numpy as jnp
from jax import lax
from jax.experimental import pallas as pl
from jax.experimental.pallas import tpu as pltpu
from jax.sharding import PartitionSpec as P

epsilon = 1e-05
outer_momentum = 0.9
outer_rate = 0.7

Y, Z, C = 2, 32, 2
VMEM = pl.BlockSpec(memory_space=pltpu.VMEM)
SMEM = pl.BlockSpec(memory_space=pltpu.SMEM)
ANY = pl.BlockSpec(memory_space=pl.ANY)


def at(y, z, c):
    return (y * Z + z % Z) * C + c


def sources():
    return [(y, z, c) for y in range(Y) for z in range(Z) for c in range(C)]


def send(array, step):
    return lax.ppermute(array, "fsdp", [(at(*here), at(*step(*here))) for here in sources()])


def along_z(array, hop):
    return send(array, lambda y, z, c: (y, z + (hop if c == 0 else -hop), c))


def across_y(array):
    return send(array, lambda y, z, c: (1 - y, z, c))


def across_core(array):
    return send(array, lambda y, z, c: (y, z, 1 - c))


def chip_kernel(first, second, out):
    rows = first.shape[0]
    core = lax.rem(lax.axis_index("fsdp"), C)

    @pl.when(core == 0)
    def _():
        out[:rows, :] = second[...]
        out[rows:, :] = first[...]

    @pl.when(core != 0)
    def _():
        out[:rows, :] = first[...]
        out[rows:, :] = second[...]


def chip_rows(own):
    first = send(own, lambda y, z, c: (y, z - 1, 1) if c == 0 else (y, z, 0))
    second = send(own, lambda y, z, c: (y, z - c, c))
    rows, width = own.shape
    return pl.pallas_call(
        chip_kernel,
        out_shape=jax.ShapeDtypeStruct((C * rows, width), own.dtype),
        in_specs=[VMEM] * 2,
        out_specs=VMEM,
        compiler_params=pltpu.CompilerParams(vmem_limit_bytes=2**20),
    )(first, second)


def join_kernel(parts, *refs):
    out, first = refs[-1], 0
    for part in refs[:parts]:
        out[first : first + part.shape[0], :] = part[...]
        first += part.shape[0]


def join(parts, *ahead, flops=0):
    rows = sum(part.shape[0] for part in parts)
    width = parts[0].shape[1]
    return pl.pallas_call(
        functools.partial(join_kernel, len(parts)),
        out_shape=jax.ShapeDtypeStruct((rows, width), parts[0].dtype),
        in_specs=[VMEM] * len(parts) + [ANY] * len(ahead),
        out_specs=VMEM,
        compiler_params=pltpu.CompilerParams(vmem_limit_bytes=4 * 2**20),
        cost_estimate=pl.CostEstimate(flops=flops, bytes_accessed=4 * rows * width, transcendentals=0),
    )(*parts, *ahead)


def pick_kernel(chosen, params, local, momentum, ahead, spread, params_row, moment_row, held, sems):
    index = chosen[0]
    group = pl.multiple_of(lax.div(index, 8) * 8, 8)
    row = lax.rem(index, 8)
    copies = [
        pltpu.make_async_copy(source.at[pl.ds(group, 8)], held.at[slot], sems.at[slot])
        for slot, source in enumerate((params, local, momentum))
    ]
    for copy in copies:
        copy.start()
    for copy in copies:
        copy.wait()
    wanted = lax.broadcasted_iota(jnp.int32, (8, 128), 0) == row

    def taken(slot, lanes):
        return jnp.sum(jnp.where(wanted, held[slot, :, lanes], 0.0), axis=0, keepdims=True)

    for line in range(params_row.shape[0]):
        lanes = slice(128 * line, 128 * line + 128)
        mine = taken(0, lanes)
        spread[:, line, :] = jnp.broadcast_to(mine - taken(1, lanes), (spread.shape[0], 128))
        params_row[line : line + 1, :] = mine
        moment_row[line : line + 1, :] = taken(2, lanes)


def pick(fragment, params, local, momentum, replicas, ahead):
    length = params.shape[1]
    lines = length // 128
    row = jax.ShapeDtypeStruct((lines, 128), jnp.float32)
    return pl.pallas_call(
        pick_kernel,
        out_shape=(jax.ShapeDtypeStruct((replicas, lines, 128), jnp.float32), row, row),
        in_specs=[SMEM] + [ANY] * 4,
        out_specs=(VMEM,) * 3,
        scratch_shapes=[pltpu.VMEM((3, 8, length), jnp.float32), pltpu.SemaphoreType.DMA((3,))],
        compiler_params=pltpu.CompilerParams(vmem_limit_bytes=4 * 2**20),
    )(fragment, params, local, momentum, ahead)


def side_kernel(everyone, params_row, moment_row, tokens, params_next, moment_next, inv):
    count = everyone.shape[0]
    total = everyone[0]
    for replica in range(1, count):
        total = total + everyone[replica]
    pseudo = total / count
    moment = outer_momentum * moment_row[...] + pseudo
    moment_next[...] = moment
    params_next[...] = params_row[...] - outer_rate * (pseudo + outer_momentum * moment)
    features = tokens.shape[1]
    squares = jnp.zeros(inv.shape, jnp.float32)
    for first in range(0, features, 512):
        floated = tokens[:, first : first + 512].astype(jnp.float32)
        squares = squares + jnp.sum(floated * floated, axis=1, keepdims=True)
    inv[...] = lax.rsqrt(squares / features + epsilon)


def side(everyone, params_row, moment_row, tokens):
    row = jax.ShapeDtypeStruct(params_row.shape, jnp.float32)
    return pl.pallas_call(
        side_kernel,
        out_shape=(row, row, jax.ShapeDtypeStruct((tokens.shape[0], 1), jnp.float32)),
        in_specs=[VMEM] * 4,
        out_specs=(VMEM,) * 3,
        compiler_params=pltpu.CompilerParams(vmem_limit_bytes=4 * 2**20),
    )(everyone, params_row, moment_row, tokens)


def position():
    place = lax.axis_index("fsdp")
    chip = lax.div(place, C)
    return lax.div(chip, Z), lax.rem(chip, Z), lax.rem(place, C)


def put(piece, full, rows, other_core, offsets):
    _, z, core = position()
    owner_core = 1 - core if other_core else core
    for slot, moved in enumerate(offsets):
        owner_z = lax.rem(z + Z + jnp.where(owner_core == 0, -moved, moved + 1), Z)
        start = pl.multiple_of(owner_z * rows, rows)
        full[pl.ds(start, rows), :] = piece[slot * rows : (slot + 1) * rows, :]


def lanes_of(column, half, first, chunk):
    return pl.ds(pl.multiple_of(column * half + first, 128), chunk)


CHUNK = 512


def forward(tokens, inv, gain, full, column, total):
    for first in range(0, full.shape[0], CHUNK):
        lanes = lanes_of(column, full.shape[0], first, CHUNK)
        unit = tokens[:, lanes].astype(jnp.float32) * inv[...]
        normed = (unit * gain[:, lanes].astype(jnp.float32)).astype(jnp.bfloat16)
        total += jnp.dot(normed, full[first : first + CHUNK, :], preferred_element_type=jnp.float32)
    return total


def gained_of(upstream, gain, full, column, first):
    grad = lax.dot_general(
        upstream, full[first : first + CHUNK, :], (((1,), (1,)), ((), ())), preferred_element_type=jnp.float32
    )
    return grad * gain[:, lanes_of(column, full.shape[0], first, CHUNK)].astype(jnp.float32)


def own_kernel(rows, layout, *refs):
    pieces = refs[: len(layout)]
    tokens, inv, gain, upstream, partial, gained, full = refs[len(layout) :]
    for piece, (other_core, offsets) in zip(pieces, layout):
        put(piece, full, rows, other_core, offsets)
    y, _, _ = position()
    partial[...] = forward(tokens, inv, gain, full, y, jnp.zeros(partial.shape, jnp.float32))
    for first in range(0, full.shape[0], CHUNK):
        gained[:, first : first + CHUNK] = gained_of(upstream[...], gain, full, y, first)


def other_kernel(rows, layout, *refs):
    pieces = refs[: len(layout)]
    tokens, inv, gain, upstream, partial, gained, projected, token_grad, full, made, sems = refs[len(layout) :]
    for piece, (other_core, offsets) in zip(pieces, layout):
        put(piece, full, rows, other_core, offsets)
    y, _, _ = position()
    total = forward(tokens, inv, gain, full, 1 - y, partial[...])
    projected[...] = total.astype(jnp.bfloat16)
    above = upstream[...]
    inner = jnp.sum(above.astype(jnp.float32) * total, axis=1, keepdims=True) / tokens.shape[1]

    def finish(column, first, values):
        lanes = lanes_of(column, full.shape[0], first, CHUNK)
        unit = tokens[:, lanes].astype(jnp.float32) * inv[...]
        made[:, lanes] = (inv[...] * (values - unit * inner)).astype(jnp.bfloat16)
        copy = pltpu.make_async_copy(made.at[:, lanes], token_grad.at[:, lanes], sems.at[len(copies)])
        copy.start()
        copies.append(copy)

    copies = []
    for first in range(0, full.shape[0], CHUNK):
        finish(y, first, gained[:, first : first + CHUNK])
        finish(1 - y, first, gained_of(above, gain, full, 1 - y, first))
    for copy in copies:
        copy.wait()


def shards(tokens, norm_gain, weight, cotangent, global_params, local_params, momentum, fragment):
    own = weight[0]
    rows = C * own.shape[0]
    block = tokens[0]
    one = chip_rows(own)
    spread, params_row, moment_row = pick(
        fragment, global_params, local_params[0], momentum, lax.axis_size("replica"), one
    )
    everyone = lax.all_to_all(spread, "replica", 0, 0)
    next_one = along_z(one, 8)
    two = join((one, next_one), spread, flops=10**10)
    next_two = along_z(two, 4)
    early = along_z(two, 2)
    global_next, momentum_next, inv = side(everyone, params_row, moment_row, block)
    late = along_z(next_two, 2)
    four = join((two, next_two), inv)
    four_y = across_y(four)
    next_four = join((early, late), flops=10**10)
    next_four_y = across_y(next_four)
    eight = join((four, next_four))
    last = along_z(eight, 1)
    eight_c = across_core(eight)
    eight_y = join((four_y, next_four_y))
    last_y = along_z(eight_y, 1)
    before = (0, 8, 4, 12, 2, 10, 6, 14)
    behind = tuple(moved + 1 for moved in before)
    count, features = block.shape
    width = own.shape[1]
    half = features // Y
    layout = [(False, before), (True, before), (False, behind), (True, behind)]
    scratch = [pltpu.VMEM((half, width), jnp.bfloat16)]
    params = pltpu.CompilerParams(vmem_limit_bytes=8 * 2**20)
    flops = 2 * count * features * width
    cost = pl.CostEstimate(flops=flops, bytes_accessed=4 * 2**20, transcendentals=0)
    partial, gained = pl.pallas_call(
        functools.partial(own_kernel, rows, layout),
        out_shape=(
            jax.ShapeDtypeStruct((count, width), jnp.float32),
            jax.ShapeDtypeStruct((count, half), jnp.float32),
        ),
        in_specs=[VMEM] * (len(layout) + 4),
        out_specs=(VMEM, VMEM),
        scratch_shapes=scratch,
        compiler_params=params,
        cost_estimate=cost,
    )(eight, eight_c, last, across_core(last), block, inv, norm_gain, cotangent[0])
    projected, token_grad = pl.pallas_call(
        functools.partial(other_kernel, rows, layout),
        out_shape=(
            jax.ShapeDtypeStruct((count, width), jnp.bfloat16),
            jax.ShapeDtypeStruct((count, features), jnp.bfloat16),
        ),
        in_specs=[VMEM] * (len(layout) + 6),
        out_specs=(VMEM, ANY),
        scratch_shapes=[
            *scratch,
            pltpu.VMEM((count, features), jnp.bfloat16),
            pltpu.SemaphoreType.DMA((features // CHUNK,)),
        ],
        compiler_params=params,
        cost_estimate=cost,
    )(
        *(eight_y, across_core(eight_y), last_y, across_core(last_y)),
        *(block, inv, norm_gain, cotangent[0], partial, gained),
    )
    return (projected[None], token_grad[None], global_next.reshape(-1), momentum_next.reshape(-1))


def solution(mesh):
    placed = (
        P("replica", "fsdp", None),
        P("replica", None),
        P("replica", "fsdp", None),
        P("replica", "fsdp", None),
        P(None, "fsdp"),
        P("replica", None, "fsdp"),
        P(None, "fsdp"),
        P(),
    )
    return jax.shard_map(
        shards,
        mesh=mesh,
        in_specs=placed,
        out_specs=(P("replica", "fsdp", None), P("replica", "fsdp", None), P("fsdp"), P("fsdp")),
        check_vma=False,
    )
```
